32 devices in a mesh: prompt: 4 (over y, x), tensor: 8 (over z, core).
Axes of the slice: x: 2, y: 2, z: 4, core: 2. Of those that a mesh axis runs over, the one named last changes fastest.
Arguments:
- tokens: bfloat16 [4, 128, 8192], P('prompt')
- gate_weight: bfloat16 [8192, 28672], P('prompt', 'tensor'), may hold values from -0.0625 to 0.0625
- up_weight: bfloat16 [8192, 28672], P('prompt', 'tensor'), may hold values from -0.0625 to 0.0625
- down_weight: bfloat16 [28672, 8192], P('tensor', 'prompt')
- norm_gain: float32 [8192], P('prompt'), may hold values from 0.1 to 1.9
- unembed: bfloat16 [8192, 86016], P('prompt', 'tensor'), may hold values from -0.5 to 0.5
- guidance: float32 [4], replicated, may hold values from -1.5 to 2.5
- logit_bias: float32 [128, 86016], P('prompt', 'tensor'), may hold values from -2 to 322
Outputs:
- log_probs: float32 [128, 86016], P('prompt', 'tensor')
The draws below stay inside these ranges and needn't reach their ends.
All inputs are finite; a program needn't handle non-finite values.
Results may differ from the reference program's by a relative error of at most 0.0025.
Values may be sent and summed in bfloat16 or wider, within the bound.
A program may use at most 192 MiB of HBM per device.

```python
import jax
import jax.numpy as jnp
from jax import lax

D = 8192
FF = 28672
VOCAB = 86016
R = 128
VARIANTS = 4


def draw_tokens(key, part):
    keys = jax.random.split(key, 3)
    base = jax.random.normal(keys[0], (VARIANTS, R, D), jnp.float32)
    row_scale = 10.0 ** jax.random.uniform(keys[1], (VARIANTS, R, 1), jnp.float32)
    position = jnp.arange(D, dtype=jnp.float32).reshape(1, 1, D) / D
    column_scale = 10.0 ** (0.5 * position + 0.5 * jax.random.uniform(keys[2], (1, 1, D), jnp.float32))
    return (0.1 * base * row_scale * column_scale).astype(jnp.bfloat16)


def draw_down_weight(key, part):
    keys = jax.random.split(key, 2)
    base = jax.random.normal(keys[0], (FF, D), jnp.float32)
    position = jnp.arange(D, dtype=jnp.float32).reshape(1, D) / D
    column_scale = 10.0 ** (0.5 * position) * jax.random.uniform(keys[1], (1, D), jnp.float32, 0.5, 1.5)
    return (0.6 * base * column_scale / FF ** 0.5).astype(jnp.bfloat16)


def draw_logit_bias(key, part):
    keys = jax.random.split(key, 1)
    base = jax.random.uniform(keys[0], (R, VOCAB), jnp.float32, -2.0, 2.0)
    return base.astype(jnp.float32)


def steps_of(stream_key, extent, cuts, least, largest):
    def one(axis_at, blocks):
        steps = jax.random.uniform(jax.random.fold_in(jax.random.fold_in(stream_key, 6), axis_at), (blocks,), jnp.float32, least / len(cuts), largest / len(cuts))
        return jnp.repeat(jnp.exp(steps), extent[axis_at] // blocks).reshape((-1,) + (1,) * (len(extent) - axis_at - 1))

    gain = one(*cuts[0])
    for cut in cuts[1:]:
        gain = gain * one(*cut)
    return gain


def normal_values(key, shape, deviation, bound, cuts=(), held_as=jnp.bfloat16):
    result = jax.random.normal(key, shape, jnp.float32) * deviation
    if len(cuts) > 0:
        result = steps_of(key, shape, cuts, -0.22, 0.18) * result
    return jnp.clip(result, min=-bound, max=bound).astype(held_as)


def setup_inputs(seed: int = 0) -> dict:
    key_list = jax.random.split(jax.random.key(seed), 9)
    return {
        "tokens": draw_tokens(jax.random.fold_in(key_list[8], 71), 0),
        "gate_weight": normal_values(key_list[1], (D, FF), D ** -0.5, 0.0625, ((0, 4), (1, 8))),
        "up_weight": normal_values(key_list[2], (D, FF), D ** -0.5, 0.0625, ((0, 4), (1, 8))),
        "down_weight": draw_down_weight(jax.random.fold_in(key_list[8], 71), 0),
        "norm_gain": jnp.clip(1.0 + 0.18 * jax.random.normal(key_list[4], (D,), jnp.float32), 0.1, 1.9),
        "unembed": normal_values(key_list[5], (D, VOCAB), (3.0 / D ** 0.5), 0.5, ((0, 4), (1, 8))),
        "guidance": jnp.clip(jax.random.uniform(key_list[6], (VARIANTS,), jnp.float32, -1.5, 2.5), -1.5, 2.5),
        "logit_bias": draw_logit_bias(jax.random.fold_in(key_list[8], 71), 0),
    }


def reference(tokens, gate_weight, up_weight, down_weight, norm_gain, unembed, guidance, logit_bias):
    flat = tokens.reshape(VARIANTS * R, D)
    gate = jnp.dot(flat, gate_weight, preferred_element_type=jnp.float32)
    up = jnp.dot(flat, up_weight, preferred_element_type=jnp.float32)
    hidden = (jax.nn.silu(gate) * up).astype(jnp.bfloat16)
    branch = jnp.dot(hidden, down_weight, preferred_element_type=jnp.float32)
    state = flat.astype(jnp.float32) + branch
    mean_square = lax.optimization_barrier(jnp.mean(state * state, axis=1, keepdims=True))
    normed = (state * lax.rsqrt(mean_square + 1e-05) * norm_gain).astype(jnp.bfloat16)
    guided = jnp.zeros((R, VOCAB), jnp.float32)
    for variant in range(VARIANTS):
        rows_now = normed[variant * R:(variant + 1) * R]
        guided = guided + guidance[variant] * jnp.dot(rows_now, unembed, preferred_element_type=jnp.float32)
    scores = guided + logit_bias
    return jax.nn.log_softmax(scores, axis=1)
```

```python
import functools

import jax
import jax.numpy as jnp
from jax import lax
from jax.experimental import pallas as pl
from jax.experimental.pallas import tpu as pltpu
from jax.sharding import PartitionSpec as P

MESH = pl.DeviceIdType.MESH
F32 = jnp.float32
BF16 = jnp.bfloat16


def step_of(size, most):
    step = most
    while size % step:
        step //= 2
    return step


def greet(axes):
    barrier = pltpu.get_barrier_semaphore()
    count = 0
    for axis, n in axes:
        me = lax.axis_index(axis)
        for d in range(1, n):
            pl.semaphore_signal(barrier, inc=1, device_id={axis: lax.rem(me + d, n)}, device_id_type=MESH)
            count += 1
    pl.semaphore_wait(barrier, count)


def ffn_kernel(
    n, x_ref, gate_hbm, up_hbm, down_hbm, out_ref,
    wg, wu, wd, part, send, recv, own, hid, acc,
    w_sem, d_sem, ps_sem, pr_sem, hs_sem, hr_sem,
):
    me = lax.axis_index("prompt")
    rows, share = x_ref.shape[1:]
    steps, chunk = hid.shape[0], hid.shape[3]

    def weights(k, slot):
        at = pl.ds(pl.multiple_of(k * chunk, chunk), chunk)
        return (
            pltpu.make_async_copy(gate_hbm.at[:, at], wg.at[slot], w_sem.at[slot, 0]),
            pltpu.make_async_copy(up_hbm.at[:, at], wu.at[slot], w_sem.at[slot, 1]),
        )

    def down(k, slot):
        at = pl.ds(pl.multiple_of(k * chunk, chunk), chunk)
        return pltpu.make_async_copy(down_hbm.at[at, :], wd.at[slot], d_sem.at[slot])

    def send_part(k, d):
        q = lax.rem(me + d, n)
        return pltpu.make_async_remote_copy(
            src_ref=send.at[k, q], dst_ref=recv.at[k, d - 1],
            send_sem=ps_sem.at[k, d - 1], recv_sem=pr_sem.at[k, d - 1],
            device_id={"prompt": q}, device_id_type=MESH,
        )

    def send_hid(k, d, owner):
        q = lax.rem(me + d, n)
        return pltpu.make_async_remote_copy(
            src_ref=hid.at[k, owner], dst_ref=hid.at[k, owner],
            send_sem=hs_sem.at[k, d - 1], recv_sem=hr_sem.at[k, d - 1],
            device_id={"prompt": q}, device_id_type=MESH,
        )

    for copy in weights(0, 0):
        copy.start()
    down(0, 0).start()
    greet([("prompt", n)])

    @pl.loop(0, steps)
    def _(k):
        slot = lax.rem(k, 2)
        for copy in weights(k, slot):
            copy.wait()

        @pl.when(k + 1 < steps)
        def _():
            for copy in weights(k + 1, 1 - slot):
                copy.start()

        x = x_ref[...].reshape(n * rows, share)
        part[:, :, :chunk] = jnp.dot(x, wg[slot], preferred_element_type=F32).reshape(n, rows, chunk)
        part[:, :, chunk:] = jnp.dot(x, wu[slot], preferred_element_type=F32).reshape(n, rows, chunk)
        send[k] = part[...].astype(BF16)
        own[k] = part[me]
        for d in range(1, n):
            send_part(k, d).start()

    @pl.loop(0, steps)
    def _(k):
        for d in range(1, n):
            send_part(k, d).wait_recv()
        total = own[k]
        for d in range(1, n):
            total = total + recv[k, d - 1].astype(F32)
        gate = total[:, :chunk]
        hid[k, me] = (gate / (1.0 + jnp.exp(-gate)) * total[:, chunk:]).astype(BF16)
        for d in range(1, n):
            send_hid(k, d, me).start()

    acc[...] = jnp.zeros_like(acc)
    tile = step_of(share, 512)

    @pl.loop(0, steps)
    def _(k):
        slot = lax.rem(k, 2)
        down(k, slot).wait()

        @pl.when(k + 1 < steps)
        def _():
            down(k + 1, 1 - slot).start()

        for d in range(1, n):
            send_hid(k, d, lax.rem(me + n - d, n)).wait_recv()
        h = hid[k].reshape(n * rows, chunk)
        for t in range(share // tile):
            at = slice(t * tile, (t + 1) * tile)
            acc[:, at] += jnp.dot(h, wd[slot, :, at], preferred_element_type=F32)

    out_ref[...] = acc[...].astype(BF16)

    @pl.loop(0, steps)
    def _(k):
        for d in range(1, n):
            send_part(k, d).wait_send()
            send_hid(k, d, me).wait_send()


def ffn(n, x, gate_weight, up_weight, down_weight):
    rows, share = x.shape[1:]
    width = gate_weight.shape[1]
    chunk = step_of(width, 256)
    steps = width // chunk
    dma = pltpu.SemaphoreType.DMA
    hbm = pl.BlockSpec(memory_space=pl.ANY)
    vmem = pl.BlockSpec(memory_space=pltpu.VMEM)
    return pl.pallas_call(
        functools.partial(ffn_kernel, n),
        out_shape=jax.ShapeDtypeStruct((n * rows, share), BF16),
        in_specs=[vmem, hbm, hbm, hbm],
        out_specs=vmem,
        scratch_shapes=[
            pltpu.VMEM((2, share, chunk), BF16),
            pltpu.VMEM((2, share, chunk), BF16),
            pltpu.VMEM((2, chunk, share), BF16),
            pltpu.VMEM((n, rows, 2 * chunk), F32),
            pltpu.VMEM((steps, n, rows, 2 * chunk), BF16),
            pltpu.VMEM((steps, n - 1, rows, 2 * chunk), BF16),
            pltpu.VMEM((steps, rows, 2 * chunk), F32),
            pltpu.VMEM((steps, n, rows, chunk), BF16),
            pltpu.VMEM((n * rows, share), F32),
            dma((2, 2)),
            dma((2,)),
            dma((steps, n - 1)),
            dma((steps, n - 1)),
            dma((steps, n - 1)),
            dma((steps, n - 1)),
        ],
        compiler_params=pltpu.CompilerParams(
            collective_id=0, has_side_effects=True, vmem_limit_bytes=56 * 1024 * 1024
        ),
        name="ffn",
    )(x, gate_weight, up_weight, down_weight)


def head_kernel(
    n, m, x_ref, unembed_hbm, bias_ref, out_ref,
    w, send, recv, own, mine, stats,
    w_sem, ps_sem, pr_sem, ss_sem, sr_sem,
):
    me = lax.axis_index("prompt")
    tp = lax.axis_index("tensor")
    steps, _, rows, chunk = send.shape
    slots = w.shape[0]

    def columns(k):
        return pl.ds(pl.multiple_of(k * chunk, chunk), chunk)

    def weights(k):
        slot = lax.rem(k, slots)
        return pltpu.make_async_copy(unembed_hbm.at[:, columns(k)], w.at[slot], w_sem.at[slot])

    def send_part(k, d):
        q = lax.rem(me + d, n)
        return pltpu.make_async_remote_copy(
            src_ref=send.at[k, q], dst_ref=recv.at[k, d - 1],
            send_sem=ps_sem.at[k, d - 1], recv_sem=pr_sem.at[k, d - 1],
            device_id={"prompt": q}, device_id_type=MESH,
        )

    def send_stats(d):
        return pltpu.make_async_remote_copy(
            src_ref=mine, dst_ref=stats.at[d - 1],
            send_sem=ss_sem.at[d - 1], recv_sem=sr_sem.at[d - 1],
            device_id={"tensor": lax.rem(tp + d, m)}, device_id_type=MESH,
        )

    for k in range(slots - 1):
        weights(k).start()
    greet([("prompt", n), ("tensor", m)])

    @pl.loop(0, steps)
    def _(k):
        weights(k).wait()

        @pl.when(k + slots - 1 < steps)
        def _():
            weights(k + slots - 1).start()

        product = jnp.dot(x_ref[...], w[lax.rem(k, slots)], preferred_element_type=F32)
        own[...] = product.reshape(n, rows, chunk)
        send[k] = own[...].astype(BF16)
        out_ref[:, columns(k)] = own[me]
        for d in range(1, n):
            send_part(k, d).start()

    def gather(k, top):
        for d in range(1, n):
            send_part(k, d).wait_recv()
        total = out_ref[:, columns(k)]
        for d in range(1, n):
            total = total + recv[k, d - 1].astype(F32)
        total = total + bias_ref[:, columns(k)]
        out_ref[:, columns(k)] = total
        return jnp.maximum(top, jnp.max(total, axis=1, keepdims=True))

    top = lax.fori_loop(0, steps, gather, jnp.full((rows, 1), -jnp.inf, F32))

    def expsum(k, total):
        return total + jnp.sum(jnp.exp(out_ref[:, columns(k)] - top), axis=1, keepdims=True)

    total = lax.fori_loop(0, steps, expsum, jnp.zeros((rows, 1), F32))
    mine[0] = jnp.broadcast_to(top, (rows, 128))
    mine[1] = jnp.broadcast_to(total, (rows, 128))
    for d in range(1, m):
        send_stats(d).start()
    best = mine[0]
    for d in range(1, m):
        send_stats(d).wait_recv()
        best = jnp.maximum(best, stats[d - 1, 0])
    grand = mine[1] * jnp.exp(mine[0] - best)
    for d in range(1, m):
        grand = grand + stats[d - 1, 1] * jnp.exp(stats[d - 1, 0] - best)
    shift = (best + jnp.log(grand))[:, :1]

    @pl.loop(0, steps)
    def _(k):
        out_ref[:, columns(k)] = out_ref[:, columns(k)] - shift
        for d in range(1, n):
            send_part(k, d).wait_send()

    for d in range(1, m):
        send_stats(d).wait_send()


def head(n, m, mixed, unembed, bias):
    share, width = unembed.shape
    rows = mixed.shape[0] // n
    chunk = step_of(width, 512)
    steps = width // chunk
    dma = pltpu.SemaphoreType.DMA
    hbm = pl.BlockSpec(memory_space=pl.ANY)
    vmem = pl.BlockSpec(memory_space=pltpu.VMEM)
    return pl.pallas_call(
        functools.partial(head_kernel, n, m),
        out_shape=jax.ShapeDtypeStruct((rows, width), F32),
        in_specs=[vmem, hbm, vmem],
        out_specs=vmem,
        scratch_shapes=[
            pltpu.VMEM((4, share, chunk), BF16),
            pltpu.VMEM((steps, n, rows, chunk), BF16),
            pltpu.VMEM((steps, n - 1, rows, chunk), BF16),
            pltpu.VMEM((n, rows, chunk), F32),
            pltpu.VMEM((2, rows, 128), F32),
            pltpu.VMEM((m - 1, 2, rows, 128), F32),
            dma((4,)),
            dma((steps, n - 1)),
            dma((steps, n - 1)),
            dma((m - 1,)),
            dma((m - 1,)),
        ],
        compiler_params=pltpu.CompilerParams(
            collective_id=1, has_side_effects=True, vmem_limit_bytes=48 * 1024 * 1024
        ),
        name="head",
    )(mixed, unembed, bias)


def mid_kernel(
    n, m, branch_ref, tokens_ref, gain_ref, guidance_ref, out_ref,
    pair, send, recv, state, sums, others,
    p_sem, s_sem, r_sem, qs_sem, qr_sem, os_sem, or_sem, f_sem,
):
    me = lax.axis_index("prompt")
    tp = lax.axis_index("tensor")
    chips = m // 2
    chip, core = tp // 2, lax.rem(tp, 2)
    share = gain_ref.shape[1]
    rows = state.shape[0]
    mine = rows // n

    def at_chip(d):
        return lax.rem(chip + d, chips)

    def to_pair(c):
        return pltpu.make_async_remote_copy(
            src_ref=branch_ref.at[2 * c + 1 - core], dst_ref=pair.at[c],
            send_sem=p_sem.at[0, c], recv_sem=p_sem.at[1, c],
            device_id={"tensor": 2 * chip + 1 - core}, device_id_type=MESH,
        )

    def to_chip(d):
        return pltpu.make_async_remote_copy(
            src_ref=send.at[d - 1], dst_ref=recv.at[d - 1],
            send_sem=s_sem.at[d - 1], recv_sem=r_sem.at[d - 1],
            device_id={"tensor": 2 * at_chip(d) + core}, device_id_type=MESH,
        )

    def to_group(d):
        return pltpu.make_async_remote_copy(
            src_ref=sums, dst_ref=others.at[d - 1],
            send_sem=qs_sem.at[d - 1], recv_sem=qr_sem.at[d - 1],
            device_id={"prompt": lax.rem(me + d, n)}, device_id_type=MESH,
        )

    def block_out(d, owner):
        return pltpu.make_async_remote_copy(
            src_ref=out_ref.at[owner], dst_ref=out_ref.at[owner],
            send_sem=os_sem.at[d - 1], recv_sem=or_sem.at[d - 1],
            device_id={"tensor": 2 * at_chip(d) + core}, device_id_type=MESH,
        )

    def pass_on(e, owner):
        return pltpu.make_async_remote_copy(
            src_ref=out_ref.at[owner], dst_ref=out_ref.at[owner],
            send_sem=f_sem.at[0, e], recv_sem=f_sem.at[1, e],
            device_id={"tensor": 2 * chip + 1 - core}, device_id_type=MESH,
        )

    barrier = pltpu.get_barrier_semaphore()
    pl.semaphore_signal(barrier, inc=1, device_id={"tensor": 2 * chip + 1 - core}, device_id_type=MESH)
    for d in range(1, chips):
        pl.semaphore_signal(barrier, inc=1, device_id={"tensor": 2 * at_chip(d) + core}, device_id_type=MESH)
    for d in range(1, n):
        pl.semaphore_signal(barrier, inc=1, device_id={"prompt": lax.rem(me + d, n)}, device_id_type=MESH)
    pl.semaphore_wait(barrier, 1 + chips - 1 + n - 1)

    order = list(range(1, chips)) + [0]
    for d in order:
        to_pair(at_chip(d)).start()
    for d in range(1, chips):
        c = at_chip(d)
        to_pair(c).wait_recv()
        send[d - 1] = (branch_ref[2 * c + core].astype(F32) + pair[c].astype(F32)).astype(BF16)
        to_chip(d).start()
    to_pair(chip).wait_recv()
    state[...] = (
        tokens_ref[tp].astype(F32) + branch_ref[tp].astype(F32) + pair[chip].astype(F32)
    )
    for d in range(1, chips):
        to_chip(d).wait_recv()
        state[...] += recv[d - 1].astype(F32)
    square = jnp.sum(state[...] * state[...], axis=1, keepdims=True)
    sums[...] = jnp.broadcast_to(square, (rows, 128))
    for d in range(1, n):
        to_group(d).start()
    grand = sums[...]
    for d in range(1, n):
        to_group(d).wait_recv()
        grand = grand + others[d - 1]
    weight = lax.rsqrt(grand / (share * n) + 1e-05) * guidance_ref[...]
    sums_now = state[...] * weight[:, :1]
    mixed = sums_now[:mine]
    for v in range(1, n):
        mixed = mixed + sums_now[v * mine : (v + 1) * mine]
    out_ref[tp, :mine, :] = (mixed * gain_ref[...]).astype(BF16)
    for d in range(1, chips):
        block_out(d, tp).start()
    pass_on(0, tp).start()
    for d in range(1, chips):
        owner = 2 * lax.rem(chip + chips - d, chips) + core
        block_out(d, owner).wait_recv()
        pass_on(d, owner).start()
    for d in range(chips):
        owner = 2 * lax.rem(chip + chips - d, chips) + 1 - core
        pass_on(d, owner).wait_recv()
    for d in range(chips):
        to_pair(d).wait_send()
        pass_on(d, tp).wait_send()
        if d:
            to_chip(d).wait_send()
            block_out(d, tp).wait_send()
    for d in range(1, n):
        to_group(d).wait_send()


def middle(n, m, branch, tokens, gain, guidance):
    _, rows, share = branch.shape
    chips = m // 2
    held = max(rows // n, 16)
    dma = pltpu.SemaphoreType.DMA
    vmem = pl.BlockSpec(memory_space=pltpu.VMEM)
    return pl.pallas_call(
        functools.partial(mid_kernel, n, m),
        out_shape=jax.ShapeDtypeStruct((m, held, share), BF16),
        in_specs=[vmem] * 4,
        out_specs=vmem,
        scratch_shapes=[
            pltpu.VMEM((chips, rows, share), BF16),
            pltpu.VMEM((chips - 1, rows, share), BF16),
            pltpu.VMEM((chips - 1, rows, share), BF16),
            pltpu.VMEM((rows, share), F32),
            pltpu.VMEM((rows, 128), F32),
            pltpu.VMEM((n - 1, rows, 128), F32),
            dma((2, chips)),
            dma((chips - 1,)),
            dma((chips - 1,)),
            dma((n - 1,)),
            dma((n - 1,)),
            dma((chips - 1,)),
            dma((chips - 1,)),
            dma((2, chips)),
        ],
        compiler_params=pltpu.CompilerParams(
            collective_id=2, has_side_effects=True, vmem_limit_bytes=40 * 1024 * 1024
        ),
        name="middle",
    )(branch, tokens, gain, guidance)


def local(tokens, gate_weight, up_weight, down_weight, norm_gain, unembed, guidance, logit_bias):
    variants = lax.axis_size("prompt")
    shards = lax.axis_size("tensor")
    rows = tokens.shape[1]
    share = gate_weight.shape[0]
    spread = lax.all_to_all(tokens, "prompt", split_axis=2, concat_axis=0, tiled=True)
    partial_branch = ffn(variants, spread, gate_weight, up_weight, down_weight)
    mine = rows // shards

    def by_owner(x):
        x = x.reshape(variants, shards, mine, share).swapaxes(0, 1)
        return x.reshape(shards, variants * mine, share)

    weight = jnp.broadcast_to(jnp.repeat(guidance, mine)[:, None], (variants * mine, 128))
    mixed = middle(
        variants, shards, by_owner(partial_branch), by_owner(spread), norm_gain[None, :], weight
    )
    mixed = mixed[:, :mine].reshape(rows, share)
    return head(variants, shards, mixed, unembed, logit_bias)


def solution(mesh):
    return jax.shard_map(
        local,
        mesh=mesh,
        in_specs=(
            P("prompt", None, None),
            P("prompt", "tensor"),
            P("prompt", "tensor"),
            P("tensor", "prompt"),
            P("prompt"),
            P("prompt", "tensor"),
            P(),
            P("prompt", "tensor"),
        ),
        out_specs=P("prompt", "tensor"),
        check_vma=False,
    )
```

```python
import functools

import jax
import jax.numpy as jnp
from jax import lax
from jax.experimental import pallas as pl
from jax.experimental.pallas import tpu as pltpu
from jax.sharding import PartitionSpec as P

MESH = pl.DeviceIdType.MESH
F32 = jnp.float32
BF16 = jnp.bfloat16


def step_of(size, most):
    step = most
    while size % step:
        step //= 2
    return step


def greet(axes):
    barrier = pltpu.get_barrier_semaphore()
    count = 0
    for axis, n in axes:
        me = lax.axis_index(axis)
        for d in range(1, n):
            pl.semaphore_signal(barrier, inc=1, device_id={axis: lax.rem(me + d, n)}, device_id_type=MESH)
            count += 1
    pl.semaphore_wait(barrier, count)


def ffn_kernel(
    n, x_ref, gate_hbm, up_hbm, down_hbm, out_ref,
    wg, wu, wd, part, send, recv, own, hid, acc,
    w_sem, d_sem, ps_sem, pr_sem, hs_sem, hr_sem,
):
    me = lax.axis_index("prompt")
    rows, share = x_ref.shape[1:]
    steps, chunk = hid.shape[0], hid.shape[3]

    def weights(k, slot):
        at = pl.ds(pl.multiple_of(k * chunk, chunk), chunk)
        return (
            pltpu.make_async_copy(gate_hbm.at[:, at], wg.at[slot], w_sem.at[slot, 0]),
            pltpu.make_async_copy(up_hbm.at[:, at], wu.at[slot], w_sem.at[slot, 1]),
        )

    def down(k, slot):
        at = pl.ds(pl.multiple_of(k * chunk, chunk), chunk)
        return pltpu.make_async_copy(down_hbm.at[at, :], wd.at[slot], d_sem.at[slot])

    def send_part(k, d):
        q = lax.rem(me + d, n)
        return pltpu.make_async_remote_copy(
            src_ref=send.at[k, q], dst_ref=recv.at[k, d - 1],
            send_sem=ps_sem.at[k, d - 1], recv_sem=pr_sem.at[k, d - 1],
            device_id={"prompt": q}, device_id_type=MESH,
        )

    def send_hid(k, d, owner):
        q = lax.rem(me + d, n)
        return pltpu.make_async_remote_copy(
            src_ref=hid.at[k, owner], dst_ref=hid.at[k, owner],
            send_sem=hs_sem.at[k, d - 1], recv_sem=hr_sem.at[k, d - 1],
            device_id={"prompt": q}, device_id_type=MESH,
        )

    for copy in weights(0, 0):
        copy.start()
    down(0, 0).start()
    greet([("prompt", n)])

    @pl.loop(0, steps)
    def _(k):
        slot = lax.rem(k, 2)
        for copy in weights(k, slot):
            copy.wait()

        @pl.when(k + 1 < steps)
        def _():
            for copy in weights(k + 1, 1 - slot):
                copy.start()

        x = x_ref[...].reshape(n * rows, share)
        part[:, :, :chunk] = jnp.dot(x, wg[slot], preferred_element_type=F32).reshape(n, rows, chunk)
        part[:, :, chunk:] = jnp.dot(x, wu[slot], preferred_element_type=F32).reshape(n, rows, chunk)
        send[k] = part[...].astype(BF16)
        own[k] = part[me]
        for d in range(1, n):
            send_part(k, d).start()

    @pl.loop(0, steps)
    def _(k):
        for d in range(1, n):
            send_part(k, d).wait_recv()
        total = own[k]
        for d in range(1, n):
            total = total + recv[k, d - 1].astype(F32)
        gate = total[:, :chunk]
        hid[k, me] = (gate / (1.0 + jnp.exp(-gate)) * total[:, chunk:]).astype(BF16)
        for d in range(1, n):
            send_hid(k, d, me).start()

    acc[...] = jnp.zeros_like(acc)
    tile = step_of(share, 512)

    @pl.loop(0, steps)
    def _(k):
        slot = lax.rem(k, 2)
        down(k, slot).wait()

        @pl.when(k + 1 < steps)
        def _():
            down(k + 1, 1 - slot).start()

        for d in range(1, n):
            send_hid(k, d, lax.rem(me + n - d, n)).wait_recv()
        h = hid[k].reshape(n * rows, chunk)
        for t in range(share // tile):
            at = slice(t * tile, (t + 1) * tile)
            acc[:, at] += jnp.dot(h, wd[slot, :, at], preferred_element_type=F32)

    out_ref[...] = acc[...].astype(BF16)

    @pl.loop(0, steps)
    def _(k):
        for d in range(1, n):
            send_part(k, d).wait_send()
            send_hid(k, d, me).wait_send()


def ffn(n, x, gate_weight, up_weight, down_weight):
    rows, share = x.shape[1:]
    width = gate_weight.shape[1]
    chunk = step_of(width, 256)
    steps = width // chunk
    dma = pltpu.SemaphoreType.DMA
    hbm = pl.BlockSpec(memory_space=pl.ANY)
    vmem = pl.BlockSpec(memory_space=pltpu.VMEM)
    return pl.pallas_call(
        functools.partial(ffn_kernel, n),
        out_shape=jax.ShapeDtypeStruct((n * rows, share), BF16),
        in_specs=[vmem, hbm, hbm, hbm],
        out_specs=vmem,
        scratch_shapes=[
            pltpu.VMEM((2, share, chunk), BF16),
            pltpu.VMEM((2, share, chunk), BF16),
            pltpu.VMEM((2, chunk, share), BF16),
            pltpu.VMEM((n, rows, 2 * chunk), F32),
            pltpu.VMEM((steps, n, rows, 2 * chunk), BF16),
            pltpu.VMEM((steps, n - 1, rows, 2 * chunk), BF16),
            pltpu.VMEM((steps, rows, 2 * chunk), F32),
            pltpu.VMEM((steps, n, rows, chunk), BF16),
            pltpu.VMEM((n * rows, share), F32),
            dma((2, 2)),
            dma((2,)),
            dma((steps, n - 1)),
            dma((steps, n - 1)),
            dma((steps, n - 1)),
            dma((steps, n - 1)),
        ],
        compiler_params=pltpu.CompilerParams(
            collective_id=0, has_side_effects=True, vmem_limit_bytes=56 * 1024 * 1024
        ),
        name="ffn",
    )(x, gate_weight, up_weight, down_weight)


def flip(me, mask):
    low, high = lax.rem(me, 2), me // 2
    if mask == 1:
        return me + 1 - 2 * low
    if mask == 2:
        return me + 2 - 4 * high
    return 3 - me


def partners(me, k):
    one, two = flip(me, 1), flip(me, 2)
    odd = lax.rem(k, 2)
    return one + odd * (two - one), two + odd * (one - two)


def ffn4_kernel(
    tokens_hbm, gate_hbm, up_hbm, down_hbm, out_ref, x_ref,
    wg, wu, wd, part, send, recv, send2, recv2, own, hid, acc,
    w_sem, d_sem, t_sem, ts_sem, tr_sem, tf_sem,
    as_sem, ar_sem, bs_sem, br_sem, hs_sem, hr_sem,
):
    n = 4
    me = lax.axis_index("prompt")
    tp = lax.axis_index("tensor")
    core = lax.rem(tp, 2)
    other_core = tp + 1 - 2 * core
    rows, share = x_ref.shape[1:]
    half = rows // 2
    steps, chunk = hid.shape[0], hid.shape[3]
    diagonal = flip(me, 3)

    def weights(k, slot):
        at = pl.ds(pl.multiple_of(k * chunk, chunk), chunk)
        return (
            pltpu.make_async_copy(gate_hbm.at[:, at], wg.at[slot], w_sem.at[slot, 0]),
            pltpu.make_async_copy(up_hbm.at[:, at], wu.at[slot], w_sem.at[slot, 1]),
        )

    def down(k, slot):
        at = pl.ds(pl.multiple_of(k * chunk, chunk), chunk)
        return pltpu.make_async_copy(down_hbm.at[at, :], wd.at[slot], d_sem.at[slot])

    def columns(q):
        return pl.ds(pl.multiple_of(q * share, share), share)

    my_half = pl.ds(pl.multiple_of(core * half, half), half)
    other_half = pl.ds(pl.multiple_of((1 - core) * half, half), half)

    def tokens_to(d):
        q = lax.rem(me + d, n)
        return pltpu.make_async_remote_copy(
            src_ref=tokens_hbm.at[my_half, columns(q)], dst_ref=x_ref.at[me, my_half],
            send_sem=ts_sem.at[d - 1], recv_sem=tr_sem.at[d - 1],
            device_id={"prompt": q}, device_id_type=MESH,
        )

    def tokens_over(d, at):
        v = lax.rem(me + n - d, n)
        return pltpu.make_async_remote_copy(
            src_ref=x_ref.at[v, at], dst_ref=x_ref.at[v, at],
            send_sem=tf_sem.at[0, d - 1], recv_sem=tf_sem.at[1, d - 1],
            device_id={"tensor": other_core}, device_id_type=MESH,
        )

    def to_first(k):
        return pltpu.make_async_remote_copy(
            src_ref=send.at[k], dst_ref=recv.at[k],
            send_sem=as_sem.at[k], recv_sem=ar_sem.at[k],
            device_id={"prompt": partners(me, k)[0]}, device_id_type=MESH,
        )

    def to_second(k):
        return pltpu.make_async_remote_copy(
            src_ref=send2.at[k], dst_ref=recv2.at[k],
            send_sem=bs_sem.at[k], recv_sem=br_sem.at[k],
            device_id={"prompt": partners(me, k)[1]}, device_id_type=MESH,
        )

    def hid_to(k, which, owner, to):
        return pltpu.make_async_remote_copy(
            src_ref=hid.at[k, owner], dst_ref=hid.at[k, owner],
            send_sem=hs_sem.at[k, which], recv_sem=hr_sem.at[k, which],
            device_id={"prompt": to}, device_id_type=MESH,
        )

    for copy in weights(0, 0):
        copy.start()
    down(0, 0).start()
    keep = pltpu.make_async_copy(tokens_hbm.at[:, columns(me)], x_ref.at[me], t_sem.at[0])
    keep.start()
    barrier = pltpu.get_barrier_semaphore()
    for d in range(1, n):
        pl.semaphore_signal(barrier, inc=1, device_id={"prompt": lax.rem(me + d, n)}, device_id_type=MESH)
    pl.semaphore_signal(barrier, inc=1, device_id={"tensor": other_core}, device_id_type=MESH)
    pl.semaphore_wait(barrier, n)
    for d in range(1, n):
        tokens_to(d).start()
    for d in range(1, n):
        tokens_to(d).wait_recv()
        tokens_over(d, my_half).start()
    keep.wait()
    for d in range(1, n):
        tokens_over(d, other_half).wait_recv()

    @pl.loop(0, steps)
    def _(k):
        slot = lax.rem(k, 2)
        for copy in weights(k, slot):
            copy.wait()

        @pl.when(k + 1 < steps)
        def _():
            for copy in weights(k + 1, 1 - slot):
                copy.start()

        x = x_ref[...].reshape(n * rows, share)
        part[:, :, :chunk] = jnp.dot(x, wg[slot], preferred_element_type=F32).reshape(n, rows, chunk)
        part[:, :, chunk:] = jnp.dot(x, wu[slot], preferred_element_type=F32).reshape(n, rows, chunk)
        first, second = partners(me, k)
        send[k, 0] = part[diagonal].astype(BF16)
        send[k, 1] = part[first].astype(BF16)
        to_first(k).start()
        own[k, 0] = part[second]
        own[k, 1] = part[me]

    @pl.loop(0, steps)
    def _(k):
        to_first(k).wait_recv()
        send2[k] = (own[k, 0] + recv[k, 0].astype(F32)).astype(BF16)
        to_second(k).start()

    @pl.loop(0, steps)
    def _(k):
        first, second = partners(me, k)
        to_second(k).wait_recv()
        total = own[k, 1] + recv[k, 1].astype(F32) + recv2[k].astype(F32)
        gate = total[:, :chunk]
        hid[k, me] = (gate / (1.0 + jnp.exp(-gate)) * total[:, chunk:]).astype(BF16)
        hid_to(k, 0, me, first).start()
        hid_to(k, 1, me, second).start()

    @pl.loop(0, steps)
    def _(k):
        first, second = partners(me, k)
        hid_to(k, 0, first, first).wait_recv()
        hid_to(k, 2, first, second).start()

    acc[...] = jnp.zeros_like(acc)
    tile = step_of(share, 512)

    @pl.loop(0, steps)
    def _(k):
        slot = lax.rem(k, 2)
        first, second = partners(me, k)
        down(k, slot).wait()

        @pl.when(k + 1 < steps)
        def _():
            down(k + 1, 1 - slot).start()

        hid_to(k, 1, second, second).wait_recv()
        hid_to(k, 2, diagonal, second).wait_recv()
        h = hid[k].reshape(n * rows, chunk)
        for t in range(share // tile):
            at = slice(t * tile, (t + 1) * tile)
            acc[:, at] += jnp.dot(h, wd[slot, :, at], preferred_element_type=F32)

    out_ref[...] = acc[...].astype(BF16)

    for d in range(1, n):
        tokens_to(d).wait_send()
        tokens_over(d, my_half).wait_send()

    @pl.loop(0, steps)
    def _(k):
        first, second = partners(me, k)
        to_first(k).wait_send()
        to_second(k).wait_send()
        hid_to(k, 0, me, first).wait_send()
        hid_to(k, 1, me, second).wait_send()
        hid_to(k, 2, first, second).wait_send()


def ffn4(tokens, gate_weight, up_weight, down_weight):
    n = 4
    rows = tokens.shape[0]
    share, width = gate_weight.shape
    chunk = step_of(width, 256)
    steps = width // chunk
    dma = pltpu.SemaphoreType.DMA
    hbm = pl.BlockSpec(memory_space=pl.ANY)
    vmem = pl.BlockSpec(memory_space=pltpu.VMEM)
    return pl.pallas_call(
        ffn4_kernel,
        out_shape=(
            jax.ShapeDtypeStruct((n * rows, share), BF16),
            jax.ShapeDtypeStruct((n, rows, share), BF16),
        ),
        in_specs=[hbm, hbm, hbm, hbm],
        out_specs=(vmem, vmem),
        scratch_shapes=[
            pltpu.VMEM((2, share, chunk), BF16),
            pltpu.VMEM((2, share, chunk), BF16),
            pltpu.VMEM((2, chunk, share), BF16),
            pltpu.VMEM((n, rows, 2 * chunk), F32),
            pltpu.VMEM((steps, 2, rows, 2 * chunk), BF16),
            pltpu.VMEM((steps, 2, rows, 2 * chunk), BF16),
            pltpu.VMEM((steps, rows, 2 * chunk), BF16),
            pltpu.VMEM((steps, rows, 2 * chunk), BF16),
            pltpu.VMEM((steps, 2, rows, 2 * chunk), F32),
            pltpu.VMEM((steps, n, rows, chunk), BF16),
            pltpu.VMEM((n * rows, share), F32),
            dma((2, 2)),
            dma((2,)),
            dma((1,)),
            dma((n - 1,)),
            dma((n - 1,)),
            dma((2, n - 1)),
            dma((steps,)),
            dma((steps,)),
            dma((steps,)),
            dma((steps,)),
            dma((steps, 3)),
            dma((steps, 3)),
        ],
        compiler_params=pltpu.CompilerParams(
            collective_id=0, has_side_effects=True, vmem_limit_bytes=56 * 1024 * 1024
        ),
        name="ffn4",
    )(tokens, gate_weight, up_weight, down_weight)


def head_kernel(
    n, m, x_ref, unembed_hbm, bias_ref, out_ref,
    w, send, recv, send2, recv2, keep, own, mine, stats,
    w_sem, ps_sem, pr_sem, bs_sem, br_sem, ss_sem, sr_sem,
):
    me = lax.axis_index("prompt")
    tp = lax.axis_index("tensor")
    steps, _, rows, chunk = send.shape
    paired = n == 4
    slots = w.shape[0]

    def columns(k):
        return pl.ds(pl.multiple_of(k * chunk, chunk), chunk)

    def weights(k):
        slot = lax.rem(k, slots)
        return pltpu.make_async_copy(unembed_hbm.at[:, columns(k)], w.at[slot], w_sem.at[slot])

    def send_part(k, d):
        q = lax.rem(me + d, n)
        return pltpu.make_async_remote_copy(
            src_ref=send.at[k, q], dst_ref=recv.at[k, d - 1],
            send_sem=ps_sem.at[k, d - 1], recv_sem=pr_sem.at[k, d - 1],
            device_id={"prompt": q}, device_id_type=MESH,
        )

    def to_first(k):
        return pltpu.make_async_remote_copy(
            src_ref=send.at[k], dst_ref=recv.at[k],
            send_sem=ps_sem.at[k, 0], recv_sem=pr_sem.at[k, 0],
            device_id={"prompt": partners(me, k)[0]}, device_id_type=MESH,
        )

    def to_second(k):
        return pltpu.make_async_remote_copy(
            src_ref=send2.at[k], dst_ref=recv2.at[k],
            send_sem=bs_sem.at[k], recv_sem=br_sem.at[k],
            device_id={"prompt": partners(me, k)[1]}, device_id_type=MESH,
        )

    def send_stats(d):
        return pltpu.make_async_remote_copy(
            src_ref=mine, dst_ref=stats.at[d - 1],
            send_sem=ss_sem.at[d - 1], recv_sem=sr_sem.at[d - 1],
            device_id={"tensor": lax.rem(tp + d, m)}, device_id_type=MESH,
        )

    for k in range(slots - 1):
        weights(k).start()
    greet([("prompt", n), ("tensor", m)])

    @pl.loop(0, steps)
    def _(k):
        weights(k).wait()

        @pl.when(k + slots - 1 < steps)
        def _():
            weights(k + slots - 1).start()

        product = jnp.dot(x_ref[...], w[lax.rem(k, slots)], preferred_element_type=F32)
        own[...] = product.reshape(n, rows, chunk)
        out_ref[:, columns(k)] = own[me]
        if paired:
            first, second = partners(me, k)
            send[k, 0] = own[flip(me, 3)].astype(BF16)
            send[k, 1] = own[first].astype(BF16)
            keep[k] = own[second]
            to_first(k).start()
        else:
            send[k] = own[...].astype(BF16)
            for d in range(1, n):
                send_part(k, d).start()

    if paired:

        @pl.loop(0, steps)
        def _(k):
            to_first(k).wait_recv()
            send2[k] = (keep[k] + recv[k, 0].astype(F32)).astype(BF16)
            to_second(k).start()

    def gather(k, top):
        total = out_ref[:, columns(k)]
        if paired:
            to_second(k).wait_recv()
            total = total + recv[k, 1].astype(F32) + recv2[k].astype(F32)
        else:
            for d in range(1, n):
                send_part(k, d).wait_recv()
            for d in range(1, n):
                total = total + recv[k, d - 1].astype(F32)
        total = total + bias_ref[:, columns(k)]
        out_ref[:, columns(k)] = total
        return jnp.maximum(top, jnp.max(total, axis=1, keepdims=True))

    top = lax.fori_loop(0, steps, gather, jnp.full((rows, 1), -jnp.inf, F32))

    def expsum(k, total):
        return total + jnp.sum(jnp.exp(out_ref[:, columns(k)] - top), axis=1, keepdims=True)

    total = lax.fori_loop(0, steps, expsum, jnp.zeros((rows, 1), F32))
    mine[0] = jnp.broadcast_to(top, (rows, 128))
    mine[1] = jnp.broadcast_to(total, (rows, 128))
    for d in range(1, m):
        send_stats(d).start()
    best = mine[0]
    for d in range(1, m):
        send_stats(d).wait_recv()
        best = jnp.maximum(best, stats[d - 1, 0])
    grand = mine[1] * jnp.exp(mine[0] - best)
    for d in range(1, m):
        grand = grand + stats[d - 1, 1] * jnp.exp(stats[d - 1, 0] - best)
    shift = (best + jnp.log(grand))[:, :1]

    @pl.loop(0, steps)
    def _(k):
        out_ref[:, columns(k)] = out_ref[:, columns(k)] - shift
        if paired:
            to_first(k).wait_send()
            to_second(k).wait_send()
        else:
            for d in range(1, n):
                send_part(k, d).wait_send()

    for d in range(1, m):
        send_stats(d).wait_send()


def head(n, m, mixed, unembed, bias):
    share, width = unembed.shape
    rows = mixed.shape[0] // n
    chunk = step_of(width, 512)
    steps = width // chunk
    sent, got, extra = (2, 2, steps) if n == 4 else (n, n - 1, 1)
    dma = pltpu.SemaphoreType.DMA
    hbm = pl.BlockSpec(memory_space=pl.ANY)
    vmem = pl.BlockSpec(memory_space=pltpu.VMEM)
    return pl.pallas_call(
        functools.partial(head_kernel, n, m),
        out_shape=jax.ShapeDtypeStruct((rows, width), F32),
        in_specs=[vmem, hbm, vmem],
        out_specs=vmem,
        scratch_shapes=[
            pltpu.VMEM((4, share, chunk), BF16),
            pltpu.VMEM((steps, sent, rows, chunk), BF16),
            pltpu.VMEM((steps, got, rows, chunk), BF16),
            pltpu.VMEM((extra, rows, chunk), BF16),
            pltpu.VMEM((extra, rows, chunk), BF16),
            pltpu.VMEM((extra, rows, chunk), F32),
            pltpu.VMEM((n, rows, chunk), F32),
            pltpu.VMEM((2, rows, 128), F32),
            pltpu.VMEM((m - 1, 2, rows, 128), F32),
            dma((4,)),
            dma((steps, n - 1)),
            dma((steps, n - 1)),
            dma((extra,)),
            dma((extra,)),
            dma((m - 1,)),
            dma((m - 1,)),
        ],
        compiler_params=pltpu.CompilerParams(
            collective_id=1, has_side_effects=True, vmem_limit_bytes=48 * 1024 * 1024
        ),
        name="head",
    )(mixed, unembed, bias)


def mid_kernel(
    n, m, branch_ref, tokens_ref, gain_ref, guidance_ref, out_ref,
    pair, send, recv, state, sums, others,
    p_sem, s_sem, r_sem, qs_sem, qr_sem, os_sem, or_sem, f_sem,
):
    me = lax.axis_index("prompt")
    tp = lax.axis_index("tensor")
    chips = m // 2
    chip, core = tp // 2, lax.rem(tp, 2)
    share = gain_ref.shape[1]
    rows = state.shape[0]
    mine = rows // n

    def at_chip(d):
        return lax.rem(chip + d, chips)

    def to_pair(c):
        return pltpu.make_async_remote_copy(
            src_ref=branch_ref.at[2 * c + 1 - core], dst_ref=pair.at[c],
            send_sem=p_sem.at[0, c], recv_sem=p_sem.at[1, c],
            device_id={"tensor": 2 * chip + 1 - core}, device_id_type=MESH,
        )

    def to_chip(d):
        return pltpu.make_async_remote_copy(
            src_ref=send.at[d - 1], dst_ref=recv.at[d - 1],
            send_sem=s_sem.at[d - 1], recv_sem=r_sem.at[d - 1],
            device_id={"tensor": 2 * at_chip(d) + core}, device_id_type=MESH,
        )

    def to_group(d):
        return pltpu.make_async_remote_copy(
            src_ref=sums, dst_ref=others.at[d - 1],
            send_sem=qs_sem.at[d - 1], recv_sem=qr_sem.at[d - 1],
            device_id={"prompt": lax.rem(me + d, n)}, device_id_type=MESH,
        )

    def block_out(d, owner):
        return pltpu.make_async_remote_copy(
            src_ref=out_ref.at[owner], dst_ref=out_ref.at[owner],
            send_sem=os_sem.at[d - 1], recv_sem=or_sem.at[d - 1],
            device_id={"tensor": 2 * at_chip(d) + core}, device_id_type=MESH,
        )

    def pass_on(e, owner):
        return pltpu.make_async_remote_copy(
            src_ref=out_ref.at[owner], dst_ref=out_ref.at[owner],
            send_sem=f_sem.at[0, e], recv_sem=f_sem.at[1, e],
            device_id={"tensor": 2 * chip + 1 - core}, device_id_type=MESH,
        )

    barrier = pltpu.get_barrier_semaphore()
    pl.semaphore_signal(barrier, inc=1, device_id={"tensor": 2 * chip + 1 - core}, device_id_type=MESH)
    for d in range(1, chips):
        pl.semaphore_signal(barrier, inc=1, device_id={"tensor": 2 * at_chip(d) + core}, device_id_type=MESH)
    for d in range(1, n):
        pl.semaphore_signal(barrier, inc=1, device_id={"prompt": lax.rem(me + d, n)}, device_id_type=MESH)
    pl.semaphore_wait(barrier, 1 + chips - 1 + n - 1)

    order = list(range(1, chips)) + [0]
    for d in order:
        to_pair(at_chip(d)).start()
    for d in range(1, chips):
        c = at_chip(d)
        to_pair(c).wait_recv()
        send[d - 1] = (branch_ref[2 * c + core].astype(F32) + pair[c].astype(F32)).astype(BF16)
        to_chip(d).start()
    to_pair(chip).wait_recv()
    state[...] = (
        tokens_ref[tp].astype(F32) + branch_ref[tp].astype(F32) + pair[chip].astype(F32)
    )
    for d in range(1, chips):
        to_chip(d).wait_recv()
        state[...] += recv[d - 1].astype(F32)
    square = jnp.sum(state[...] * state[...], axis=1, keepdims=True)
    sums[...] = jnp.broadcast_to(square, (rows, 128))
    for d in range(1, n):
        to_group(d).start()
    grand = sums[...]
    for d in range(1, n):
        to_group(d).wait_recv()
        grand = grand + others[d - 1]
    weight = lax.rsqrt(grand / (share * n) + 1e-05) * guidance_ref[...]
    sums_now = state[...] * weight[:, :1]
    mixed = sums_now[:mine]
    for v in range(1, n):
        mixed = mixed + sums_now[v * mine : (v + 1) * mine]
    out_ref[tp, :mine, :] = (mixed * gain_ref[...]).astype(BF16)
    for d in range(1, chips):
        block_out(d, tp).start()
    pass_on(0, tp).start()
    for d in range(1, chips):
        owner = 2 * lax.rem(chip + chips - d, chips) + core
        block_out(d, owner).wait_recv()
        pass_on(d, owner).start()
    for d in range(chips):
        owner = 2 * lax.rem(chip + chips - d, chips) + 1 - core
        pass_on(d, owner).wait_recv()
    for d in range(chips):
        to_pair(d).wait_send()
        pass_on(d, tp).wait_send()
        if d:
            to_chip(d).wait_send()
            block_out(d, tp).wait_send()
    for d in range(1, n):
        to_group(d).wait_send()


def middle(n, m, branch, tokens, gain, guidance):
    _, rows, share = branch.shape
    chips = m // 2
    held = max(rows // n, 16)
    dma = pltpu.SemaphoreType.DMA
    vmem = pl.BlockSpec(memory_space=pltpu.VMEM)
    return pl.pallas_call(
        functools.partial(mid_kernel, n, m),
        out_shape=jax.ShapeDtypeStruct((m, held, share), BF16),
        in_specs=[vmem] * 4,
        out_specs=vmem,
        scratch_shapes=[
            pltpu.VMEM((chips, rows, share), BF16),
            pltpu.VMEM((chips - 1, rows, share), BF16),
            pltpu.VMEM((chips - 1, rows, share), BF16),
            pltpu.VMEM((rows, share), F32),
            pltpu.VMEM((rows, 128), F32),
            pltpu.VMEM((n - 1, rows, 128), F32),
            dma((2, chips)),
            dma((chips - 1,)),
            dma((chips - 1,)),
            dma((n - 1,)),
            dma((n - 1,)),
            dma((chips - 1,)),
            dma((chips - 1,)),
            dma((2, chips)),
        ],
        compiler_params=pltpu.CompilerParams(
            collective_id=2, has_side_effects=True, vmem_limit_bytes=40 * 1024 * 1024
        ),
        name="middle",
    )(branch, tokens, gain, guidance)


def local(tokens, gate_weight, up_weight, down_weight, norm_gain, unembed, guidance, logit_bias):
    variants = lax.axis_size("prompt")
    shards = lax.axis_size("tensor")
    rows = tokens.shape[1]
    share = gate_weight.shape[0]
    if variants == 4:
        partial_branch, spread = ffn4(tokens[0], gate_weight, up_weight, down_weight)
    else:
        spread = lax.all_to_all(tokens, "prompt", split_axis=2, concat_axis=0, tiled=True)
        partial_branch = ffn(variants, spread, gate_weight, up_weight, down_weight)
    mine = rows // shards

    def by_owner(x):
        x = x.reshape(variants, shards, mine, share).swapaxes(0, 1)
        return x.reshape(shards, variants * mine, share)

    weight = jnp.broadcast_to(jnp.repeat(guidance, mine)[:, None], (variants * mine, 128))
    mixed = middle(
        variants, shards, by_owner(partial_branch), by_owner(spread), norm_gain[None, :], weight
    )
    mixed = mixed[:, :mine].reshape(rows, share)
    return head(variants, shards, mixed, unembed, logit_bias)


def solution(mesh):
    return jax.shard_map(
        local,
        mesh=mesh,
        in_specs=(
            P("prompt", None, None),
            P("prompt", "tensor"),
            P("prompt", "tensor"),
            P("tensor", "prompt"),
            P("prompt"),
            P("prompt", "tensor"),
            P(),
            P("prompt", "tensor"),
        ),
        out_specs=P("prompt", "tensor"),
        check_vma=False,
    )
```

```python
import functools

import jax
import jax.numpy as jnp
from jax import lax
from jax.experimental import pallas as pl
from jax.experimental.pallas import tpu as pltpu
from jax.sharding import PartitionSpec as P

MESH = pl.DeviceIdType.MESH
F32 = jnp.float32
BF16 = jnp.bfloat16


def step_of(size, most):
    step = most
    while size % step:
        step //= 2
    return step


def greet(axes):
    barrier = pltpu.get_barrier_semaphore()
    count = 0
    for axis, n in axes:
        me = lax.axis_index(axis)
        for d in range(1, n):
            pl.semaphore_signal(barrier, inc=1, device_id={axis: lax.rem(me + d, n)}, device_id_type=MESH)
            count += 1
    pl.semaphore_wait(barrier, count)


def ffn_kernel(
    n, x_ref, gate_hbm, up_hbm, down_hbm, out_ref,
    wg, wu, wd, part, send, recv, own, hid, acc,
    w_sem, d_sem, ps_sem, pr_sem, hs_sem, hr_sem,
):
    me = lax.axis_index("prompt")
    rows, share = x_ref.shape[1:]
    steps, chunk = hid.shape[0], hid.shape[3]

    def weights(k, slot):
        at = pl.ds(pl.multiple_of(k * chunk, chunk), chunk)
        return (
            pltpu.make_async_copy(gate_hbm.at[:, at], wg.at[slot], w_sem.at[slot, 0]),
            pltpu.make_async_copy(up_hbm.at[:, at], wu.at[slot], w_sem.at[slot, 1]),
        )

    def down(k, slot):
        at = pl.ds(pl.multiple_of(k * chunk, chunk), chunk)
        return pltpu.make_async_copy(down_hbm.at[at, :], wd.at[slot], d_sem.at[slot])

    def send_part(k, d):
        q = lax.rem(me + d, n)
        return pltpu.make_async_remote_copy(
            src_ref=send.at[k, q], dst_ref=recv.at[k, d - 1],
            send_sem=ps_sem.at[k, d - 1], recv_sem=pr_sem.at[k, d - 1],
            device_id={"prompt": q}, device_id_type=MESH,
        )

    def send_hid(k, d, owner):
        q = lax.rem(me + d, n)
        return pltpu.make_async_remote_copy(
            src_ref=hid.at[k, owner], dst_ref=hid.at[k, owner],
            send_sem=hs_sem.at[k, d - 1], recv_sem=hr_sem.at[k, d - 1],
            device_id={"prompt": q}, device_id_type=MESH,
        )

    for copy in weights(0, 0):
        copy.start()
    down(0, 0).start()
    greet([("prompt", n)])

    @pl.loop(0, steps)
    def _(k):
        slot = lax.rem(k, 2)
        for copy in weights(k, slot):
            copy.wait()

        @pl.when(k + 1 < steps)
        def _():
            for copy in weights(k + 1, 1 - slot):
                copy.start()

        x = x_ref[...].reshape(n * rows, share)
        part[:, :, :chunk] = jnp.dot(x, wg[slot], preferred_element_type=F32).reshape(n, rows, chunk)
        part[:, :, chunk:] = jnp.dot(x, wu[slot], preferred_element_type=F32).reshape(n, rows, chunk)
        send[k] = part[...].astype(BF16)
        own[k] = part[me]
        for d in range(1, n):
            send_part(k, d).start()

    @pl.loop(0, steps)
    def _(k):
        for d in range(1, n):
            send_part(k, d).wait_recv()
        total = own[k]
        for d in range(1, n):
            total = total + recv[k, d - 1].astype(F32)
        gate = total[:, :chunk]
        hid[k, me] = (gate / (1.0 + jnp.exp(-gate)) * total[:, chunk:]).astype(BF16)
        for d in range(1, n):
            send_hid(k, d, me).start()

    acc[...] = jnp.zeros_like(acc)
    tile = step_of(share, 512)

    @pl.loop(0, steps)
    def _(k):
        slot = lax.rem(k, 2)
        down(k, slot).wait()

        @pl.when(k + 1 < steps)
        def _():
            down(k + 1, 1 - slot).start()

        for d in range(1, n):
            send_hid(k, d, lax.rem(me + n - d, n)).wait_recv()
        h = hid[k].reshape(n * rows, chunk)
        for t in range(share // tile):
            at = slice(t * tile, (t + 1) * tile)
            acc[:, at] += jnp.dot(h, wd[slot, :, at], preferred_element_type=F32)

    out_ref[...] = acc[...].astype(BF16)

    @pl.loop(0, steps)
    def _(k):
        for d in range(1, n):
            send_part(k, d).wait_send()
            send_hid(k, d, me).wait_send()


def ffn(n, x, gate_weight, up_weight, down_weight):
    rows, share = x.shape[1:]
    width = gate_weight.shape[1]
    chunk = step_of(width, 256)
    steps = width // chunk
    dma = pltpu.SemaphoreType.DMA
    hbm = pl.BlockSpec(memory_space=pl.ANY)
    vmem = pl.BlockSpec(memory_space=pltpu.VMEM)
    return pl.pallas_call(
        functools.partial(ffn_kernel, n),
        out_shape=jax.ShapeDtypeStruct((n * rows, share), BF16),
        in_specs=[vmem, hbm, hbm, hbm],
        out_specs=vmem,
        scratch_shapes=[
            pltpu.VMEM((2, share, chunk), BF16),
            pltpu.VMEM((2, share, chunk), BF16),
            pltpu.VMEM((2, chunk, share), BF16),
            pltpu.VMEM((n, rows, 2 * chunk), F32),
            pltpu.VMEM((steps, n, rows, 2 * chunk), BF16),
            pltpu.VMEM((steps, n - 1, rows, 2 * chunk), BF16),
            pltpu.VMEM((steps, rows, 2 * chunk), F32),
            pltpu.VMEM((steps, n, rows, chunk), BF16),
            pltpu.VMEM((n * rows, share), F32),
            dma((2, 2)),
            dma((2,)),
            dma((steps, n - 1)),
            dma((steps, n - 1)),
            dma((steps, n - 1)),
            dma((steps, n - 1)),
        ],
        compiler_params=pltpu.CompilerParams(
            collective_id=0, has_side_effects=True, vmem_limit_bytes=56 * 1024 * 1024
        ),
        name="ffn",
    )(x, gate_weight, up_weight, down_weight)


def flip(me, mask):
    low, high = lax.rem(me, 2), me // 2
    if mask == 1:
        return me + 1 - 2 * low
    if mask == 2:
        return me + 2 - 4 * high
    return 3 - me


def partners(me, k):
    one, two = flip(me, 1), flip(me, 2)
    odd = lax.rem(k, 2)
    return one + odd * (two - one), two + odd * (one - two)


def ffn4_kernel(
    tokens_hbm, gate_hbm, up_hbm, down_hbm, out_ref, mine_ref,
    x_ref, wg, wu, wd, part, send, recv, send2, recv2, own, hid, acc,
    w_sem, d_sem, t_sem, ts_sem, tr_sem, tf_sem,
    as_sem, ar_sem, bs_sem, br_sem, hs_sem, hr_sem,
):
    n = 4
    me = lax.axis_index("prompt")
    tp = lax.axis_index("tensor")
    core = lax.rem(tp, 2)
    other_core = tp + 1 - 2 * core
    rows, share = x_ref.shape[1:]
    half = rows // 2
    steps, chunk = hid.shape[0], hid.shape[3]
    diagonal = flip(me, 3)

    def weights(k, slot):
        at = pl.ds(pl.multiple_of(k * chunk, chunk), chunk)
        return (
            pltpu.make_async_copy(gate_hbm.at[:, at], wg.at[slot], w_sem.at[slot, 0]),
            pltpu.make_async_copy(up_hbm.at[:, at], wu.at[slot], w_sem.at[slot, 1]),
        )

    def down(k, slot):
        at = pl.ds(pl.multiple_of(k * chunk, chunk), chunk)
        return pltpu.make_async_copy(down_hbm.at[at, :], wd.at[slot], d_sem.at[slot])

    def columns(q):
        return pl.ds(pl.multiple_of(q * share, share), share)

    my_half = pl.ds(pl.multiple_of(core * half, half), half)
    other_half = pl.ds(pl.multiple_of((1 - core) * half, half), half)

    def tokens_to(d):
        q = lax.rem(me + d, n)
        return pltpu.make_async_remote_copy(
            src_ref=tokens_hbm.at[my_half, columns(q)], dst_ref=x_ref.at[me, my_half],
            send_sem=ts_sem.at[d - 1], recv_sem=tr_sem.at[d - 1],
            device_id={"prompt": q}, device_id_type=MESH,
        )

    def tokens_over(d, at):
        v = lax.rem(me + n - d, n)
        return pltpu.make_async_remote_copy(
            src_ref=x_ref.at[v, at], dst_ref=x_ref.at[v, at],
            send_sem=tf_sem.at[0, d - 1], recv_sem=tf_sem.at[1, d - 1],
            device_id={"tensor": other_core}, device_id_type=MESH,
        )

    def to_first(k):
        return pltpu.make_async_remote_copy(
            src_ref=send.at[k], dst_ref=recv.at[k],
            send_sem=as_sem.at[k], recv_sem=ar_sem.at[k],
            device_id={"prompt": partners(me, k)[0]}, device_id_type=MESH,
        )

    def to_second(k):
        return pltpu.make_async_remote_copy(
            src_ref=send2.at[k], dst_ref=recv2.at[k],
            send_sem=bs_sem.at[k], recv_sem=br_sem.at[k],
            device_id={"prompt": partners(me, k)[1]}, device_id_type=MESH,
        )

    def hid_to(k, which, owner, to):
        return pltpu.make_async_remote_copy(
            src_ref=hid.at[k, owner], dst_ref=hid.at[k, owner],
            send_sem=hs_sem.at[k, which], recv_sem=hr_sem.at[k, which],
            device_id={"prompt": to}, device_id_type=MESH,
        )

    for copy in weights(0, 0):
        copy.start()
    down(0, 0).start()
    keep = pltpu.make_async_copy(tokens_hbm.at[:, columns(me)], x_ref.at[me], t_sem.at[0])
    keep.start()
    barrier = pltpu.get_barrier_semaphore()
    for d in range(1, n):
        pl.semaphore_signal(barrier, inc=1, device_id={"prompt": lax.rem(me + d, n)}, device_id_type=MESH)
    pl.semaphore_signal(barrier, inc=1, device_id={"tensor": other_core}, device_id_type=MESH)
    pl.semaphore_wait(barrier, n)
    for d in range(1, n):
        tokens_to(d).start()
    for d in range(1, n):
        tokens_to(d).wait_recv()
        tokens_over(d, my_half).start()
    keep.wait()
    for d in range(1, n):
        tokens_over(d, other_half).wait_recv()

    @pl.loop(0, steps)
    def _(k):
        slot = lax.rem(k, 2)
        for copy in weights(k, slot):
            copy.wait()

        @pl.when(k + 1 < steps)
        def _():
            for copy in weights(k + 1, 1 - slot):
                copy.start()

        x = x_ref[...].reshape(n * rows, share)
        part[:, :, :chunk] = jnp.dot(x, wg[slot], preferred_element_type=F32).reshape(n, rows, chunk)
        part[:, :, chunk:] = jnp.dot(x, wu[slot], preferred_element_type=F32).reshape(n, rows, chunk)
        first, second = partners(me, k)
        send[k, 0] = part[diagonal].astype(BF16)
        send[k, 1] = part[first].astype(BF16)
        to_first(k).start()
        own[k, 0] = part[second]
        own[k, 1] = part[me]

    @pl.loop(0, steps)
    def _(k):
        to_first(k).wait_recv()
        send2[k] = (own[k, 0] + recv[k, 0].astype(F32)).astype(BF16)
        to_second(k).start()

    @pl.loop(0, steps)
    def _(k):
        first, second = partners(me, k)
        to_second(k).wait_recv()
        total = own[k, 1] + recv[k, 1].astype(F32) + recv2[k].astype(F32)
        gate = total[:, :chunk]
        hid[k, me] = (gate / (1.0 + jnp.exp(-gate)) * total[:, chunk:]).astype(BF16)
        hid_to(k, 0, me, first).start()
        hid_to(k, 1, me, second).start()

    @pl.loop(0, steps)
    def _(k):
        first, second = partners(me, k)
        hid_to(k, 0, first, first).wait_recv()
        hid_to(k, 2, first, second).start()

    acc[...] = jnp.zeros_like(acc)
    tile = step_of(share, 512)

    @pl.loop(0, steps)
    def _(k):
        slot = lax.rem(k, 2)
        first, second = partners(me, k)
        down(k, slot).wait()

        @pl.when(k + 1 < steps)
        def _():
            down(k + 1, 1 - slot).start()

        hid_to(k, 1, second, second).wait_recv()
        hid_to(k, 2, diagonal, second).wait_recv()
        h = hid[k].reshape(n * rows, chunk)
        for t in range(share // tile):
            at = slice(t * tile, (t + 1) * tile)
            acc[:, at] += jnp.dot(h, wd[slot, :, at], preferred_element_type=F32)

    mine = mine_ref.shape[0] // n
    my_rows = pl.ds(pl.multiple_of(tp * mine, mine), mine)
    for v in range(n):
        at = slice(v * mine, (v + 1) * mine)
        mine_ref[at, :] = x_ref[v, my_rows, :]
        for j in range(rows // mine):
            row = v * rows + j * mine
            out_ref[j, at, :] = acc[row : row + mine, :].astype(BF16)

    for d in range(1, n):
        tokens_to(d).wait_send()
        tokens_over(d, my_half).wait_send()

    @pl.loop(0, steps)
    def _(k):
        first, second = partners(me, k)
        to_first(k).wait_send()
        to_second(k).wait_send()
        hid_to(k, 0, me, first).wait_send()
        hid_to(k, 1, me, second).wait_send()
        hid_to(k, 2, first, second).wait_send()


def ffn4(m, tokens, gate_weight, up_weight, down_weight):
    n = 4
    rows = tokens.shape[0]
    share, width = gate_weight.shape
    chunk = step_of(width, 256)
    steps = width // chunk
    dma = pltpu.SemaphoreType.DMA
    hbm = pl.BlockSpec(memory_space=pl.ANY)
    vmem = pl.BlockSpec(memory_space=pltpu.VMEM)
    return pl.pallas_call(
        ffn4_kernel,
        out_shape=(
            jax.ShapeDtypeStruct((m, n * rows // m, share), BF16),
            jax.ShapeDtypeStruct((n * rows // m, share), BF16),
        ),
        in_specs=[hbm, hbm, hbm, hbm],
        out_specs=(vmem, vmem),
        scratch_shapes=[
            pltpu.VMEM((n, rows, share), BF16),
            pltpu.VMEM((2, share, chunk), BF16),
            pltpu.VMEM((2, share, chunk), BF16),
            pltpu.VMEM((2, chunk, share), BF16),
            pltpu.VMEM((n, rows, 2 * chunk), F32),
            pltpu.VMEM((steps, 2, rows, 2 * chunk), BF16),
            pltpu.VMEM((steps, 2, rows, 2 * chunk), BF16),
            pltpu.VMEM((steps, rows, 2 * chunk), BF16),
            pltpu.VMEM((steps, rows, 2 * chunk), BF16),
            pltpu.VMEM((steps, 2, rows, 2 * chunk), F32),
            pltpu.VMEM((steps, n, rows, chunk), BF16),
            pltpu.VMEM((n * rows, share), F32),
            dma((2, 2)),
            dma((2,)),
            dma((1,)),
            dma((n - 1,)),
            dma((n - 1,)),
            dma((2, n - 1)),
            dma((steps,)),
            dma((steps,)),
            dma((steps,)),
            dma((steps,)),
            dma((steps, 3)),
            dma((steps, 3)),
        ],
        compiler_params=pltpu.CompilerParams(
            collective_id=0, has_side_effects=True, vmem_limit_bytes=56 * 1024 * 1024
        ),
        name="ffn4",
    )(tokens, gate_weight, up_weight, down_weight)


def head_kernel(
    n, m, x_ref, unembed_hbm, bias_ref, out_ref,
    w, send, recv, send2, recv2, keep, own, mine, stats,
    w_sem, ps_sem, pr_sem, bs_sem, br_sem, ss_sem, sr_sem,
):
    me = lax.axis_index("prompt")
    tp = lax.axis_index("tensor")
    steps, _, rows, chunk = send.shape
    paired = n == 4
    slots = w.shape[0]

    def columns(k):
        return pl.ds(pl.multiple_of(k * chunk, chunk), chunk)

    def weights(k):
        slot = lax.rem(k, slots)
        return pltpu.make_async_copy(unembed_hbm.at[:, columns(k)], w.at[slot], w_sem.at[slot])

    def send_part(k, d):
        q = lax.rem(me + d, n)
        return pltpu.make_async_remote_copy(
            src_ref=send.at[k, q], dst_ref=recv.at[k, d - 1],
            send_sem=ps_sem.at[k, d - 1], recv_sem=pr_sem.at[k, d - 1],
            device_id={"prompt": q}, device_id_type=MESH,
        )

    def to_first(k):
        return pltpu.make_async_remote_copy(
            src_ref=send.at[k], dst_ref=recv.at[k],
            send_sem=ps_sem.at[k, 0], recv_sem=pr_sem.at[k, 0],
            device_id={"prompt": partners(me, k)[0]}, device_id_type=MESH,
        )

    def to_second(k):
        return pltpu.make_async_remote_copy(
            src_ref=send2.at[k], dst_ref=recv2.at[k],
            send_sem=bs_sem.at[k], recv_sem=br_sem.at[k],
            device_id={"prompt": partners(me, k)[1]}, device_id_type=MESH,
        )

    def send_stats(d):
        return pltpu.make_async_remote_copy(
            src_ref=mine, dst_ref=stats.at[d - 1],
            send_sem=ss_sem.at[d - 1], recv_sem=sr_sem.at[d - 1],
            device_id={"tensor": lax.rem(tp + d, m)}, device_id_type=MESH,
        )

    for k in range(slots - 1):
        weights(k).start()
    greet([("prompt", n), ("tensor", m)])

    def multiply(k):
        weights(k).wait()

        @pl.when(k + slots - 1 < steps)
        def _():
            weights(k + slots - 1).start()

        product = jnp.dot(x_ref[...], w[lax.rem(k, slots)], preferred_element_type=F32)
        own[...] = product.reshape(n, rows, chunk)
        out_ref[:, columns(k)] = own[me]
        if paired:
            first, second = partners(me, k)
            send[k, 0] = own[flip(me, 3)].astype(BF16)
            send[k, 1] = own[first].astype(BF16)
            keep[k] = own[second]
            to_first(k).start()
        else:
            send[k] = own[...].astype(BF16)
            for d in range(1, n):
                send_part(k, d).start()

    def relay(k):
        to_first(k).wait_recv()
        send2[k] = (keep[k] + recv[k, 0].astype(F32)).astype(BF16)
        to_second(k).start()

    lag = min(3, steps) if paired else 0

    @pl.loop(0, lag)
    def _(k):
        multiply(k)

    @pl.loop(lag, steps)
    def _(k):
        multiply(k)
        if paired:
            relay(k - lag)

    @pl.loop(steps - lag, steps)
    def _(k):
        relay(k)

    def gather(k, top):
        total = out_ref[:, columns(k)]
        if paired:
            to_second(k).wait_recv()
            total = total + recv[k, 1].astype(F32) + recv2[k].astype(F32)
        else:
            for d in range(1, n):
                send_part(k, d).wait_recv()
            for d in range(1, n):
                total = total + recv[k, d - 1].astype(F32)
        total = total + bias_ref[:, columns(k)]
        out_ref[:, columns(k)] = total
        return jnp.maximum(top, jnp.max(total, axis=1, keepdims=True))

    top = lax.fori_loop(0, steps, gather, jnp.full((rows, 1), -jnp.inf, F32))

    def expsum(k, total):
        return total + jnp.sum(jnp.exp(out_ref[:, columns(k)] - top), axis=1, keepdims=True)

    total = lax.fori_loop(0, steps, expsum, jnp.zeros((rows, 1), F32))
    mine[0] = jnp.broadcast_to(top, (rows, 128))
    mine[1] = jnp.broadcast_to(total, (rows, 128))
    for d in range(1, m):
        send_stats(d).start()
    best = mine[0]
    for d in range(1, m):
        send_stats(d).wait_recv()
        best = jnp.maximum(best, stats[d - 1, 0])
    grand = mine[1] * jnp.exp(mine[0] - best)
    for d in range(1, m):
        grand = grand + stats[d - 1, 1] * jnp.exp(stats[d - 1, 0] - best)
    shift = (best + jnp.log(grand))[:, :1]

    @pl.loop(0, steps)
    def _(k):
        out_ref[:, columns(k)] = out_ref[:, columns(k)] - shift
        if paired:
            to_first(k).wait_send()
            to_second(k).wait_send()
        else:
            for d in range(1, n):
                send_part(k, d).wait_send()

    for d in range(1, m):
        send_stats(d).wait_send()


def head(n, m, mixed, unembed, bias):
    share, width = unembed.shape
    rows = mixed.shape[0] // n
    chunk = step_of(width, 512)
    steps = width // chunk
    sent, got, extra = (2, 2, steps) if n == 4 else (n, n - 1, 1)
    dma = pltpu.SemaphoreType.DMA
    hbm = pl.BlockSpec(memory_space=pl.ANY)
    vmem = pl.BlockSpec(memory_space=pltpu.VMEM)
    return pl.pallas_call(
        functools.partial(head_kernel, n, m),
        out_shape=jax.ShapeDtypeStruct((rows, width), F32),
        in_specs=[vmem, hbm, vmem],
        out_specs=vmem,
        scratch_shapes=[
            pltpu.VMEM((4, share, chunk), BF16),
            pltpu.VMEM((steps, sent, rows, chunk), BF16),
            pltpu.VMEM((steps, got, rows, chunk), BF16),
            pltpu.VMEM((extra, rows, chunk), BF16),
            pltpu.VMEM((extra, rows, chunk), BF16),
            pltpu.VMEM((extra, rows, chunk), F32),
            pltpu.VMEM((n, rows, chunk), F32),
            pltpu.VMEM((2, rows, 128), F32),
            pltpu.VMEM((m - 1, 2, rows, 128), F32),
            dma((4,)),
            dma((steps, n - 1)),
            dma((steps, n - 1)),
            dma((extra,)),
            dma((extra,)),
            dma((m - 1,)),
            dma((m - 1,)),
        ],
        compiler_params=pltpu.CompilerParams(
            collective_id=1, has_side_effects=True, vmem_limit_bytes=48 * 1024 * 1024
        ),
        name="head",
    )(mixed, unembed, bias)


def mid_kernel(
    n, m, branch_ref, tokens_ref, gain_ref, guidance_ref, out_ref,
    pair, send, recv, state, sums, others,
    p_sem, s_sem, r_sem, qs_sem, qr_sem, os_sem, or_sem, f_sem,
):
    me = lax.axis_index("prompt")
    tp = lax.axis_index("tensor")
    chips = m // 2
    chip, core = tp // 2, lax.rem(tp, 2)
    share = gain_ref.shape[1]
    rows = state.shape[0]
    mine = rows // n

    def at_chip(d):
        return lax.rem(chip + d, chips)

    def to_pair(c):
        return pltpu.make_async_remote_copy(
            src_ref=branch_ref.at[2 * c + 1 - core], dst_ref=pair.at[c],
            send_sem=p_sem.at[0, c], recv_sem=p_sem.at[1, c],
            device_id={"tensor": 2 * chip + 1 - core}, device_id_type=MESH,
        )

    def to_chip(d):
        return pltpu.make_async_remote_copy(
            src_ref=send.at[d - 1], dst_ref=recv.at[d - 1],
            send_sem=s_sem.at[d - 1], recv_sem=r_sem.at[d - 1],
            device_id={"tensor": 2 * at_chip(d) + core}, device_id_type=MESH,
        )

    def to_group(d):
        return pltpu.make_async_remote_copy(
            src_ref=sums, dst_ref=others.at[d - 1],
            send_sem=qs_sem.at[d - 1], recv_sem=qr_sem.at[d - 1],
            device_id={"prompt": lax.rem(me + d, n)}, device_id_type=MESH,
        )

    def block_out(d, owner):
        return pltpu.make_async_remote_copy(
            src_ref=out_ref.at[owner], dst_ref=out_ref.at[owner],
            send_sem=os_sem.at[d - 1], recv_sem=or_sem.at[d - 1],
            device_id={"tensor": 2 * at_chip(d) + core}, device_id_type=MESH,
        )

    def pass_on(e, owner):
        return pltpu.make_async_remote_copy(
            src_ref=out_ref.at[owner], dst_ref=out_ref.at[owner],
            send_sem=f_sem.at[0, e], recv_sem=f_sem.at[1, e],
            device_id={"tensor": 2 * chip + 1 - core}, device_id_type=MESH,
        )

    barrier = pltpu.get_barrier_semaphore()
    pl.semaphore_signal(barrier, inc=1, device_id={"tensor": 2 * chip + 1 - core}, device_id_type=MESH)
    for d in range(1, chips):
        pl.semaphore_signal(barrier, inc=1, device_id={"tensor": 2 * at_chip(d) + core}, device_id_type=MESH)
    for d in range(1, n):
        pl.semaphore_signal(barrier, inc=1, device_id={"prompt": lax.rem(me + d, n)}, device_id_type=MESH)
    pl.semaphore_wait(barrier, 1 + chips - 1 + n - 1)

    order = list(range(1, chips)) + [0]
    for d in order:
        to_pair(at_chip(d)).start()
    for d in range(1, chips):
        c = at_chip(d)
        to_pair(c).wait_recv()
        send[d - 1] = (branch_ref[2 * c + core].astype(F32) + pair[c].astype(F32)).astype(BF16)
        to_chip(d).start()
    to_pair(chip).wait_recv()
    state[...] = (
        tokens_ref[...].astype(F32) + branch_ref[tp].astype(F32) + pair[chip].astype(F32)
    )
    for d in range(1, chips):
        to_chip(d).wait_recv()
        state[...] += recv[d - 1].astype(F32)
    square = jnp.sum(state[...] * state[...], axis=1, keepdims=True)
    sums[...] = jnp.broadcast_to(square, (rows, 128))
    for d in range(1, n):
        to_group(d).start()
    grand = sums[...]
    for d in range(1, n):
        to_group(d).wait_recv()
        grand = grand + others[d - 1]
    weight = lax.rsqrt(grand / (share * n) + 1e-05) * guidance_ref[...]
    sums_now = state[...] * weight[:, :1]
    mixed = sums_now[:mine]
    for v in range(1, n):
        mixed = mixed + sums_now[v * mine : (v + 1) * mine]
    out_ref[tp, :mine, :] = (mixed * gain_ref[...]).astype(BF16)
    for d in range(1, chips):
        block_out(d, tp).start()
    pass_on(0, tp).start()
    for d in range(1, chips):
        owner = 2 * lax.rem(chip + chips - d, chips) + core
        block_out(d, owner).wait_recv()
        pass_on(d, owner).start()
    for d in range(chips):
        owner = 2 * lax.rem(chip + chips - d, chips) + 1 - core
        pass_on(d, owner).wait_recv()
    for d in range(chips):
        to_pair(d).wait_send()
        pass_on(d, tp).wait_send()
        if d:
            to_chip(d).wait_send()
            block_out(d, tp).wait_send()
    for d in range(1, n):
        to_group(d).wait_send()


def middle(n, m, branch, tokens, gain, guidance):
    _, rows, share = branch.shape
    chips = m // 2
    held = max(rows // n, 16)
    dma = pltpu.SemaphoreType.DMA
    vmem = pl.BlockSpec(memory_space=pltpu.VMEM)
    return pl.pallas_call(
        functools.partial(mid_kernel, n, m),
        out_shape=jax.ShapeDtypeStruct((m, held, share), BF16),
        in_specs=[vmem] * 4,
        out_specs=vmem,
        scratch_shapes=[
            pltpu.VMEM((chips, rows, share), BF16),
            pltpu.VMEM((chips - 1, rows, share), BF16),
            pltpu.VMEM((chips - 1, rows, share), BF16),
            pltpu.VMEM((rows, share), F32),
            pltpu.VMEM((rows, 128), F32),
            pltpu.VMEM((n - 1, rows, 128), F32),
            dma((2, chips)),
            dma((chips - 1,)),
            dma((chips - 1,)),
            dma((n - 1,)),
            dma((n - 1,)),
            dma((chips - 1,)),
            dma((chips - 1,)),
            dma((2, chips)),
        ],
        compiler_params=pltpu.CompilerParams(
            collective_id=2, has_side_effects=True, vmem_limit_bytes=40 * 1024 * 1024
        ),
        name="middle",
    )(branch, tokens, gain, guidance)


def local(tokens, gate_weight, up_weight, down_weight, norm_gain, unembed, guidance, logit_bias):
    variants = lax.axis_size("prompt")
    shards = lax.axis_size("tensor")
    rows = tokens.shape[1]
    share = gate_weight.shape[0]
    mine = rows // shards
    if variants == 4:
        branch, own = ffn4(shards, tokens[0], gate_weight, up_weight, down_weight)
    else:

        def by_owner(x):
            x = x.reshape(variants, shards, mine, share).swapaxes(0, 1)
            return x.reshape(shards, variants * mine, share)

        spread = lax.all_to_all(tokens, "prompt", split_axis=2, concat_axis=0, tiled=True)
        branch = by_owner(ffn(variants, spread, gate_weight, up_weight, down_weight))
        own = lax.dynamic_index_in_dim(by_owner(spread), lax.axis_index("tensor"), 0, keepdims=False)
    weight = jnp.broadcast_to(jnp.repeat(guidance, mine)[:, None], (variants * mine, 128))
    mixed = middle(
        variants, shards, branch, own, norm_gain[None, :], weight
    )
    mixed = mixed[:, :mine].reshape(rows, share)
    return head(variants, shards, mixed, unembed, logit_bias)


def solution(mesh):
    return jax.shard_map(
        local,
        mesh=mesh,
        in_specs=(
            P("prompt", None, None),
            P("prompt", "tensor"),
            P("prompt", "tensor"),
            P("tensor", "prompt"),
            P("prompt"),
            P("prompt", "tensor"),
            P(),
            P("prompt", "tensor"),
        ),
        out_specs=P("prompt", "tensor"),
        check_vma=False,
    )
```
